256 devices in a mesh: mass: 128 (over x, z, y), rep: 2 (over core).
Axes of the slice: x: 4, y: 4, z: 8, core: 2. Of those that a mesh axis runs over, the one named last changes fastest.
Arguments:
- spectra: bfloat16 [131072, 1024], P(('mass', 'rep')), may hold values from -200 to 200
- window: int32 [131072], P(('mass', 'rep')), may hold values from 0 to 127, as said below
- labels: int32 [131072], P(('mass', 'rep')), may hold values from 0 to 63
- edge_labels: int32 [131072], P(('mass', 'rep')), may hold values from -1 to 63, as said below
Outputs:
- consensus: bfloat16 [8192, 1024], P('mass', 'rep')
- assigned: bfloat16 [131072, 1024], P(('mass', 'rep'))
The draws below stay inside these ranges and needn't reach their ends.
Inputs may be any that keep to these rules, and one draw needn't show every extreme that they name: A file shard's 512 spectra hold between 0 and 8 of any one window. At least one window, the same in every file shard, gets exactly 8 from every file shard, so a window holds at most 2048 spectra in all; other windows may get fewer. A file shard holds between 0 and 1 spectra with edge_labels >= 0 of any one window. At least one window, the same in every file shard, gets exactly 1 such spectra from every file shard, so a window holds at most 256 of them; other windows may get fewer.
All inputs are finite; a program needn't handle non-finite values.
Results may differ from the reference program's by a relative error of at most 0.0033.
Values may be sent and summed in bfloat16 or wider, within the bound.
A program may use at most 64 MiB of HBM per device.

```python
import math
import jax
import jax.numpy as jnp
from jax import lax

DIM = 1024
ROWS_DEV = 512
CLUSTERS = 64
CAP = 8
EDGE_K = 1
EDGE_CAP = 128
WINDOW_ROWS = 1024
TOKENS = 131072
N_MASS = 128


def layout(key):
    sources = TOKENS // ROWS_DEV
    slot_count = WINDOW_ROWS
    windows = slot_count // CAP
    keys = jax.random.split(key, 6)
    popular = jax.random.randint(keys[0], (windows,), 0, 4096)
    busiest = jax.random.randint(keys[1], (), 0, windows)
    slot_ids = jnp.arange(slot_count, dtype=jnp.int32)
    slot_window = slot_ids // CAP
    jitter = jax.random.randint(keys[2], (sources, slot_count), 0, 4096)
    ranking = (jitter + popular[slot_window][None, :]) * slot_count + slot_ids[None, :]
    ranking = ranking + jnp.where(slot_window == busiest, 2 ** 28, 0)[None, :]
    cover_slot = jnp.arange(sources, dtype=jnp.int32) % windows * CAP
    ranking = ranking + jnp.where(slot_ids[None, :] == cover_slot[:, None], 2 ** 27, 0)
    chosen = lax.top_k(ranking, ROWS_DEV)[1]
    mixing = jax.random.randint(keys[3], (sources, ROWS_DEV), 0, 4096) * ROWS_DEV + jnp.arange(ROWS_DEV, dtype=jnp.int32)[None, :]
    shuffled = jnp.take_along_axis(chosen, jnp.argsort(mixing, axis=1), axis=1)
    window = shuffled // CAP
    at_edge = shuffled % CAP < EDGE_K
    cluster_of = jax.random.randint(keys[4], (sources, ROWS_DEV), 0, CLUSTERS)
    edge_of = jnp.where(at_edge, jax.random.randint(keys[5], (sources, ROWS_DEV), 0, CLUSTERS), -1)
    return (window.reshape(-1), cluster_of.reshape(-1), edge_of.reshape(-1))


def draw_window(key, part):
    shared = layout(key)
    return shared[0]


def draw_labels(key, part):
    shared = layout(key)
    return shared[1]


def draw_edge_labels(key, part):
    shared = layout(key)
    return shared[2]


def draw_spectra(key, part):
    window, cluster_of, edge_of = layout(key)
    key = jax.random.fold_in(key, 4)
    keys = jax.random.split(key, 4)
    windows = WINDOW_ROWS // CAP
    centers = jax.random.truncated_normal(keys[0], -4.0, 4.0, (windows * CLUSTERS, DIM))
    own_center = centers[window * CLUSTERS + cluster_of]
    prior = jnp.clip(window - 1, 0, windows - 1) * CLUSTERS + jnp.maximum(edge_of, 0)
    strength = jnp.exp(jax.random.uniform(keys[1], (TOKENS, 1), minval=math.log(0.5), maxval=math.log(3.0)))
    pull = jnp.exp(jax.random.uniform(keys[2], (TOKENS, 1), minval=math.log(1.0), maxval=math.log(3.0)))
    pull = jnp.where(((edge_of >= 0) & (window > 0))[:, None], pull, 0.0)
    rough = jax.random.truncated_normal(keys[3], -4.0, 4.0, (TOKENS, DIM))
    values = strength * own_center + pull * centers[prior] + rough
    return values.astype(jnp.bfloat16)


def setup_inputs(seed: int = 0) -> dict:
    seeds = jax.random.split(jax.random.key(seed), 5)
    spectra = draw_spectra(jax.random.fold_in(seeds[4], 71), 0)
    window = draw_window(jax.random.fold_in(seeds[4], 71), 0)
    labels = draw_labels(jax.random.fold_in(seeds[4], 71), 0)
    edge_labels = draw_edge_labels(jax.random.fold_in(seeds[4], 71), 0)
    return dict(spectra=spectra, window=window, labels=labels, edge_labels=edge_labels)


BETA = 6.0

def reference(spectra, window, labels, edge_labels):
    widened = spectra.astype(jnp.float32)
    unit_rows = (widened * lax.rsqrt(lax.optimization_barrier(jnp.mean(widened * widened, axis=1, keepdims=True)) + 1e-06)).astype(jnp.bfloat16)
    span_rows = 2 * N_MASS * CAP
    edge_room = 2 * EDGE_CAP
    by_window = jnp.argsort(window, stable=True)
    counts = jnp.bincount(window, length=N_MASS).astype(jnp.int32)
    starts = (jnp.cumsum(counts) - counts).astype(jnp.int32)
    sorted_rows = jnp.concatenate([unit_rows[by_window], jnp.zeros((span_rows, DIM), jnp.bfloat16)], axis=0)
    sorted_labels = jnp.concatenate([labels[by_window], -jnp.ones((span_rows,), jnp.int32)], axis=0)
    sorted_edges = jnp.concatenate([edge_labels[by_window], -jnp.ones((span_rows,), jnp.int32)], axis=0)
    cluster_ids = jnp.arange(CLUSTERS, dtype=jnp.int32)
    positions = jnp.arange(span_rows, dtype=jnp.int32)

    def one_window(index):
        begin_at = starts[index]
        member_rows = lax.dynamic_slice_in_dim(sorted_rows, begin_at, span_rows, 0)
        own_labels = jnp.where(positions < counts[index], lax.dynamic_slice_in_dim(sorted_labels, begin_at, span_rows, 0), -1)
        following = jnp.minimum(index + 1, N_MASS - 1).astype(jnp.int32)
        next_count = jnp.where(index + 1 < N_MASS, counts[following], 0)
        next_rows = lax.dynamic_slice_in_dim(sorted_rows, starts[following], span_rows, 0)
        next_edges = jnp.where(positions < next_count, lax.dynamic_slice_in_dim(sorted_edges, starts[following], span_rows, 0), -1)
        edge_pick = jnp.argsort((next_edges < 0).astype(jnp.int32), stable=True)[:edge_room]
        cand_rows = jnp.concatenate([member_rows, next_rows[edge_pick]], axis=0)
        cand_labels = jnp.concatenate([own_labels, next_edges[edge_pick]], axis=0)
        scores = lax.dot_general(member_rows, cand_rows, (((1,), (1,)), ((), ())), preferred_element_type=jnp.float32) / DIM
        same_cluster = (own_labels[:, None] == cand_labels[None, :]) & (own_labels[:, None] >= 0)
        density = lax.optimization_barrier(jnp.sum(jnp.where(same_cluster, jnp.exp(BETA * (scores - 1.0)), 0.0), axis=1))
        weighted = (density[:, None] * member_rows.astype(jnp.float32)).astype(jnp.bfloat16)
        member = own_labels[None, :] == cluster_ids[:, None]
        numerator = jnp.dot(member.astype(jnp.bfloat16), weighted, preferred_element_type=jnp.float32)
        member_count = lax.optimization_barrier(jnp.sum(member.astype(jnp.float32), axis=1))
        return (numerator / (member_count + 1.0)[:, None]).astype(jnp.bfloat16)
    tables = lax.map(one_window, jnp.arange(N_MASS, dtype=jnp.int32))
    consensus = tables.reshape(N_MASS * CLUSTERS, DIM)
    assigned = consensus[window * CLUSTERS + labels]
    return (consensus, assigned)
```

```python
import functools

import jax
import jax.numpy as jnp
from jax import lax
from jax.experimental import pallas as pl
from jax.experimental.pallas import tpu as pltpu
from jax.sharding import PartitionSpec as P

MESH = pl.DeviceIdType.MESH
CLUSTERS = 64
SLOTS = 8
BETA = 6.0
F32 = jnp.float32
BF16 = jnp.bfloat16
NT = (((1,), (1,)), ((), ()))


def iota(shape, dim):
    return lax.broadcasted_iota(jnp.int32, shape, dim)


def onehot(cond):
    return jnp.where(cond, 1.0, 0.0).astype(BF16)


def mm(a, b):
    return jnp.dot(a, b, preferred_element_type=F32)


def mm_nt(a, b):
    return lax.dot_general(a, b, NT, preferred_element_type=F32)


def kernel(
    x_ref, code_ref, cons_ref, out_ref,
    unit, send, msend, own, sib, mown, msib, edge_send, edge_own, edge_sib, medge, num, num_sib, cnt, cnt_sib,
    table, ret, acc, dens, lab_col,
    send_sem, msend_sem, ret_send_sem, row_sem, meta_sem, ret_sem, pair_send, pair_recv, edge_ssem, edge_rsem, loc_sem,
):
    me = lax.axis_index("mass")
    rep = lax.axis_index("rep")
    other = 1 - rep
    n = 128
    x, z, y = me // 32, (me // 4) % 8, me % 4
    prev = lax.rem(me + n - 1, n)

    def target(d):
        dx, dz, dy = d // 32, (d // 4) % 8, d % 4
        return lax.rem(x + dx, 4) * 32 + lax.rem(z + dz, 8) * 4 + lax.rem(y + dy, 4)

    barrier = pltpu.get_barrier_semaphore()

    @pl.loop(1, n)
    def _(d):
        pl.semaphore_signal(barrier, inc=1, device_id=(target(d), rep), device_id_type=MESH)

    pl.semaphore_signal(barrier, inc=1, device_id=(me, other), device_id_type=MESH)

    wide = x_ref[...].astype(F32)
    unit[...] = (wide * lax.rsqrt(jnp.mean(wide * wide, axis=1, keepdims=True) + 1e-6)).astype(BF16)

    code_row = code_ref[...]
    rows = code_row.shape[1]
    diag = iota((rows, rows), 0) == iota((rows, rows), 1)
    code_col = jnp.sum(jnp.where(diag, code_row.astype(F32), 0.0), axis=1, keepdims=True).astype(jnp.int32)

    def fields(code):
        return code >> 13, (code >> 7) & 63, code & 127

    w_row, _, e_row = fields(code_row)
    w_col, l_col, e_col = fields(code_col)
    key_row = iota((1, rows), 1) - jnp.where(e_row > 0, rows, 0)
    key_col = iota((rows, 1), 0) - jnp.where(e_col > 0, rows, 0)
    same = w_col == w_row
    rank_row = jnp.sum(jnp.where(same & (key_col < key_row), 1.0, 0.0), axis=0, keepdims=True).astype(jnp.int32)
    rank_col = jnp.sum(jnp.where(same & (key_row < key_col), 1.0, 0.0), axis=1, keepdims=True).astype(jnp.int32)
    slot_row = w_row * SLOTS + rank_row
    slot_col = w_col * SLOTS + rank_col

    for c in range(4):
        pick = onehot(iota((256, rows), 0) + 256 * c == slot_row)
        send[pl.ds(32 * c, 32)] = mm(pick, unit[...]).reshape(32, SLOTS, 1024).astype(BF16)

    lane = iota((rows, 128), 1)
    code2 = jnp.where(lane == rank_col, l_col + 1, 0) + jnp.where(lane == rank_col + SLOTS, e_col, 0)
    meta = mm(onehot(iota((n, rows), 0) == w_row), code2.astype(F32).astype(BF16))
    msend[...] = meta.reshape(n, 1, 128)

    pl.semaphore_wait(barrier, n)

    def row_copy(t, s):
        return pltpu.make_async_remote_copy(
            src_ref=send.at[t], dst_ref=own.at[s], send_sem=send_sem, recv_sem=row_sem.at[s // 32],
            device_id=(t, rep), device_id_type=MESH)

    def meta_copy(t, s):
        return pltpu.make_async_remote_copy(
            src_ref=msend.at[t], dst_ref=mown.at[s], send_sem=msend_sem, recv_sem=meta_sem,
            device_id=(t, rep), device_id_type=MESH)

    pltpu.make_async_copy(send.at[me], own.at[me], row_sem.at[x]).start()
    pltpu.make_async_copy(msend.at[me], mown.at[me], meta_sem).start()

    @pl.loop(1, n)
    def _(d):
        t = target(d)
        row_copy(t, me).start()
        meta_copy(t, me).start()

    def pair_copy(src, dst, k):
        return pltpu.make_async_remote_copy(
            src_ref=src, dst_ref=dst, send_sem=pair_send.at[k], recv_sem=pair_recv.at[k],
            device_id=(me, other), device_id_type=MESH)

    pair_copies = []
    for q in range(4):
        s = lax.rem(x + 4 - q, 4)
        part = pl.ds(s * 32, 32)
        pltpu.make_async_copy(send.at[part], own.at[part], row_sem.at[s]).wait()
        copy = pair_copy(own.at[part], sib.at[part], q)
        copy.start()
        pair_copies.append(copy)
    pltpu.make_async_copy(msend, mown, meta_sem).wait()
    copy = pair_copy(mown, msib, 4)
    copy.start()
    pair_copies.append(copy)

    first = onehot(iota((n, n * SLOTS), 1) == SLOTS * iota((n, n * SLOTS), 0))
    own_rows = own[...].reshape(n * SLOTS, 1024)
    edge_send[...] = mm(first, own_rows).astype(BF16)
    edge_copies = [
        pltpu.make_async_remote_copy(
            src_ref=src, dst_ref=dst, send_sem=edge_ssem.at[k], recv_sem=edge_rsem.at[k],
            device_id=(prev, rep), device_id_type=MESH)
        for k, (src, dst) in enumerate([(edge_send, edge_own), (mown, medge.at[0])])
    ]
    for copy in edge_copies:
        copy.start()

    spread = onehot(iota((n * SLOTS, n), 0) // SLOTS == iota((n * SLOTS, n), 1))
    slot_lane = iota((n * SLOTS, n), 1) == iota((n * SLOTS, n), 0) % SLOTS

    def label_forms(meta_in):
        per_slot = jnp.where(slot_lane, mm(spread, meta_in.astype(BF16)), 0.0)
        col = jnp.sum(per_slot, axis=1, keepdims=True)
        row = mm_nt(jnp.ones((8, n), BF16), per_slot.astype(BF16))[0:1]
        return col, row

    col, row_own = label_forms(mown[...].reshape(n, 128))
    lab_col[...] = col

    def add_density(cand, cand_labels, begin):
        for q in range(4):
            part = pl.ds(q * 256, 256)
            scores = mm_nt(own[pl.ds(q * 32, 32)].reshape(256, 1024), cand) * (1.0 / 1024.0)
            kept = jnp.where(lab_col[part] == cand_labels, jnp.exp(BETA * (scores - 1.0)), 0.0)
            total = jnp.sum(kept, axis=1, keepdims=True)
            dens[part] = total if begin else dens[part] + total

    add_density(own_rows, row_own, True)
    for copy in pair_copies:
        copy.wait()
    _, row_sib = label_forms(msib[...].reshape(n, 128))
    for copy in edge_copies:
        copy.wait()
    relay = [pair_copy(edge_own, edge_sib, 5), pair_copy(medge.at[0], medge.at[1], 6)]
    for copy in relay:
        copy.start()
    add_density(sib[...].reshape(n * SLOTS, 1024), row_sib, False)
    edge_lane = onehot(iota((8, 128), 1) == SLOTS)
    live = me < n - 1

    def edge_labels(k):
        codes = mm_nt(edge_lane, medge[k].reshape(n, 128).astype(BF16))[0:1]
        return jnp.where(live, codes, 0.0)

    for copy in relay:
        copy.wait()
    add_density(
        jnp.concatenate([edge_own[...], edge_sib[...]], axis=0),
        jnp.concatenate([edge_labels(0), edge_labels(1)], axis=1), False)

    weighted = (dens[...] * own_rows.astype(F32)).astype(BF16)
    member = onehot(iota((CLUSTERS, n * SLOTS), 0) + 1 == row_own.astype(jnp.int32))
    num[...] = mm(member, weighted)
    cnt[...] = jnp.broadcast_to(jnp.sum(member.astype(F32), axis=1, keepdims=True), (CLUSTERS, 128))
    pair_num = [pair_copy(num, num_sib, 7), pair_copy(cnt, cnt_sib, 8)]
    for copy in pair_num:
        copy.start()
    for copy in pair_num:
        copy.wait()
    table[...] = ((num[...] + num_sib[...]) / (cnt[:, 0:1] + cnt_sib[:, 0:1] + 1.0)).astype(BF16)
    cons_ref[...] = table[:, pl.ds(pl.multiple_of(rep * 512, 512), 512)]

    pltpu.make_async_remote_copy(
        src_ref=send.at[pl.ds(0, n - 1)], dst_ref=own.at[pl.ds(0, n - 1)], send_sem=send_sem, recv_sem=row_sem.at[0],
        device_id=(me, other), device_id_type=MESH).wait_send()
    pltpu.make_async_remote_copy(
        src_ref=msend.at[pl.ds(0, n - 1)], dst_ref=mown.at[pl.ds(0, n - 1)], send_sem=msend_sem, recv_sem=meta_sem,
        device_id=(me, other), device_id_type=MESH).wait_send()

    def ret_copy(t, s):
        return pltpu.make_async_remote_copy(
            src_ref=send.at[t], dst_ref=ret.at[s], send_sem=ret_send_sem, recv_sem=ret_sem.at[s // 32],
            device_id=(t, rep), device_id_type=MESH)

    for q in range(4):
        qx = lax.rem(x + q, 4)
        part = pl.ds(pl.multiple_of(qx * 256, 256), 256)
        pick = onehot(iota((256, CLUSTERS), 1) + 1 == lab_col[part].astype(jnp.int32))
        send[pl.ds(qx * 32, 32)] = mm(pick, table[...]).reshape(32, SLOTS, 1024).astype(BF16)
        if q == 0:
            pltpu.make_async_copy(send.at[me], ret.at[me], ret_sem.at[x]).start()

        @pl.loop(max(1, 32 * q), 32 * q + 32)
        def _(d):
            ret_copy(target(d), me).start()

    for q in range(4):
        s = lax.rem(x + 4 - q, 4)
        part = pl.ds(s * 32, 32)
        pltpu.make_async_copy(send.at[part], ret.at[part], ret_sem.at[s]).wait()
        pick = onehot(iota((rows, 256), 1) + 256 * s == slot_col)
        got = mm(pick, ret[part].reshape(256, 1024))
        if q == 0:
            acc[...] = got
        elif q < 3:
            acc[...] += got
        else:
            out_ref[...] = (acc[...] + got).astype(BF16)
    pltpu.make_async_remote_copy(
        src_ref=send.at[pl.ds(0, n - 1)], dst_ref=ret.at[pl.ds(0, n - 1)], send_sem=ret_send_sem, recv_sem=ret_sem.at[0],
        device_id=(me, other), device_id_type=MESH).wait_send()


def body(spectra, window, labels, edge_labels):
    rows, dim = spectra.shape
    n = lax.axis_size("mass")
    code = (window * 8192 + labels * 128 + edge_labels + 1).reshape(1, rows)
    vm = lambda shape, t=BF16: pltpu.VMEM(shape, t)
    block = (n, SLOTS, dim)
    meta = (n, 1, 128)
    dma = pltpu.SemaphoreType.DMA
    return pl.pallas_call(
        kernel,
        out_shape=(
            jax.ShapeDtypeStruct((CLUSTERS, dim // 2), BF16),
            jax.ShapeDtypeStruct((rows, dim), BF16),
        ),
        in_specs=[pl.BlockSpec(memory_space=pltpu.VMEM)] * 2,
        out_specs=(pl.BlockSpec(memory_space=pltpu.VMEM), pl.BlockSpec(memory_space=pltpu.VMEM)),
        scratch_shapes=[
            vm((rows, dim)), vm(block), vm(meta, F32), vm(block), vm(block), vm(meta, F32), vm(meta, F32),
            vm((n, dim)), vm((n, dim)), vm((n, dim)), vm((2,) + meta, F32),
            vm((CLUSTERS, dim), F32), vm((CLUSTERS, dim), F32), vm((CLUSTERS, 128), F32), vm((CLUSTERS, 128), F32),
            vm((CLUSTERS, dim)), vm(block), vm((rows, dim), F32), vm((n * SLOTS, 1), F32), vm((n * SLOTS, 1), F32),
            dma, dma, dma, dma((4,)), dma, dma((4,)), dma((9,)), dma((9,)), dma((2,)), dma((2,)), dma,
        ],
        compiler_params=pltpu.CompilerParams(
            collective_id=0, has_side_effects=True, vmem_limit_bytes=56 * 1024 * 1024),
        cost_estimate=pl.CostEstimate(flops=8 * 10**9, bytes_accessed=4 * 10**6, transcendentals=2 * 10**6),
        name="consensus",
    )(spectra, code)


def solution(mesh):
    placed = (P(("mass", "rep"), None), P(("mass", "rep")), P(("mass", "rep")), P(("mass", "rep")))
    return jax.shard_map(
        body,
        mesh=mesh,
        in_specs=placed,
        out_specs=(P("mass", "rep"), P(("mass", "rep"), None)),
        check_vma=False,
    )
```

```python
import functools

import jax
import jax.numpy as jnp
from jax import lax
from jax.experimental import pallas as pl
from jax.experimental.pallas import tpu as pltpu
from jax.sharding import PartitionSpec as P

MESH = pl.DeviceIdType.MESH
CLUSTERS = 64
SLOTS = 8
BETA = 6.0
F32 = jnp.float32
BF16 = jnp.bfloat16
NT = (((1,), (1,)), ((), ()))


def iota(shape, dim):
    return lax.broadcasted_iota(jnp.int32, shape, dim)


def onehot(cond):
    return jnp.where(cond, 1.0, 0.0).astype(BF16)


def mm(a, b):
    return jnp.dot(a, b, preferred_element_type=F32)


def mm_nt(a, b):
    return lax.dot_general(a, b, NT, preferred_element_type=F32)


ZO = (0, 1, 7, 2, 6, 3, 5, 4)
GROUPS = ((0, 32), (32, 32), (64, 32), (96, 16), (112, 16))


def depth_of(j):
    return jnp.where(j % 2 == 1, (j + 1) // 2, (8 - j // 2) % 8)


def order_of(depth):
    return jnp.where(depth > 4, 2 * (8 - depth), jnp.maximum(2 * depth - 1, 0))


def kernel(
    x_ref, code_ref, cons_ref, out_ref,
    unit, send, own, sib, ret, acc, msend, mplane, mz, mz_sib, ztab,
    edge_send, edge_own, edge_sib, ecode_send, ecode_own, ecode_sib, num, num_sib, cnt, cnt_sib, dens, lab_col,
    line_a, line_b, row_ssem, row_sem, ret_ssem, ret_sem, mp_ssem, mp_sem, mz_ssem, mz_sem,
    pair_ssem, pair_sem, edge_ssem, edge_sem, zt_ssem, zt_sem, zp_ssem, zp_sem,
):
    me = lax.axis_index("mass")
    rep = lax.axis_index("rep")
    other = 1 - rep
    n = 128
    rows = x_ref.shape[0]
    x, z, y = me // 32, (me // 4) % 8, me % 4

    def chip(dx, dz, dy):
        return ((x + dx) % 4) * 32 + ((z + dz) % 8) * 4 + (y + dy) % 4

    def signal(sem, m, r):
        pl.semaphore_signal(sem, inc=1, device_id=(m, r), device_id_type=MESH)

    def remote(src, dst, ssem, rsem, m, r):
        return pltpu.make_async_remote_copy(
            src_ref=src, dst_ref=dst, send_sem=ssem, recv_sem=rsem, device_id=(m, r), device_id_type=MESH)

    barrier = pltpu.get_barrier_semaphore()
    for k in range(1, 8):
        signal(barrier, chip(0, k, 0), rep)
    for k in range(1, 4):
        signal(barrier, chip(k, 0, 0), rep)
        signal(barrier, chip(0, 0, k), rep)
    signal(barrier, me, other)

    code_row = code_ref[...]
    diag = iota((rows, rows), 0) == iota((rows, rows), 1)
    code_col = jnp.sum(jnp.where(diag, code_row.astype(F32), 0.0), axis=1, keepdims=True).astype(jnp.int32)

    def fields(code):
        return code >> 13, (code >> 7) & 63, code & 127

    w_row, _, e_row = fields(code_row)
    w_col, l_col, e_col = fields(code_col)
    key_row = iota((1, rows), 1) - jnp.where(e_row > 0, rows, 0)
    key_col = iota((rows, 1), 0) - jnp.where(e_col > 0, rows, 0)
    same = w_col == w_row
    rank_row = jnp.sum(jnp.where(same & (key_col < key_row), 1.0, 0.0), axis=0, keepdims=True).astype(jnp.int32)
    rank_col = jnp.sum(jnp.where(same & (key_row < key_col), 1.0, 0.0), axis=1, keepdims=True).astype(jnp.int32)

    def place(window):
        plane = (((window >> 5) - x) & 3) * 4 + ((window - y) & 3)
        return plane, order_of(((window >> 2) - z) & 7)

    plane_row, order_row = place(w_row)
    plane_col, order_col = place(w_col)
    slot_row = (plane_row * 8 + order_row) * SLOTS + rank_row
    slot_col = (order_col * 16 + plane_col) * SLOTS + rank_col

    pl.semaphore_wait(barrier, 14)
    for k in range(1, 4):
        signal(line_a, chip(0, 0, k), rep)

    wide = x_ref[...].astype(F32)
    unit[...] = (wide * lax.rsqrt(jnp.mean(wide * wide, axis=1, keepdims=True) + 1e-6)).astype(BF16)

    pl.semaphore_wait(line_a, 3)
    for k in range(1, 4):
        signal(line_b, chip(k, 0, 0), rep)

    lane = iota((rows, 128), 1) - ((w_col >> 2) & 7) * 16
    code2 = jnp.where(lane == rank_col, l_col + 1, 0) + jnp.where(lane == rank_col + SLOTS, e_col, 0)
    meta = mm(onehot(iota((16, rows), 0) == plane_row), code2.astype(F32).astype(BF16))
    msend[...] = meta.reshape(16, 1, 128)

    def pack(c):
        pick = onehot(iota((256, rows), 0) + 256 * c == slot_row)
        send[pl.ds(32 * c, 32)] = mm(pick, unit[...]).reshape(32, SLOTS, 1024).astype(BF16)

    pack(0)
    pl.semaphore_wait(line_b, 3)

    def plane_copy(p, sign):
        return remote(msend.at[p], mplane.at[p], mp_ssem, mp_sem, chip(sign * (p // 4), 0, sign * (p % 4)), rep)

    pltpu.make_async_copy(msend.at[0], mplane.at[0], mp_sem).start()
    pltpu.make_async_copy(send.at[0], own.at[0], row_sem.at[0]).start()
    for p in range(1, 16):
        plane_copy(p, 1).start()

    def send_rows(group):
        begin, count = GROUPS[group]

        @pl.loop(max(1, begin), begin + count)
        def _(d):
            p = d // 8
            m = chip(p // 4, depth_of(d % 8), p % 4)
            remote(send.at[d], own.at[d], row_ssem, row_sem.at[group], m, rep).start()

    send_rows(0)
    for c in range(1, 4):
        pack(c)
    send_rows(1)

    pltpu.make_async_copy(msend, mplane, mp_sem).wait()
    mz[0] = mplane[...].reshape(16, 128).astype(BF16)
    for j in range(1, 8):
        remote(mz.at[0], mz.at[j], mz_ssem.at[j], mz_sem.at[j], chip(0, ZO[j], 0), rep).start()
    send_rows(2)
    send_rows(3)
    send_rows(4)

    def pair(src, dst, k):
        return remote(src, dst, pair_ssem.at[k], pair_sem.at[k], me, other)

    for j in range(1, 8):
        remote(mz.at[0], mz.at[j], mz_ssem.at[j], mz_sem.at[j], chip(0, ZO[j], 0), rep).wait()
    pair_meta = pair(mz, mz_sib, 5)
    pair_meta.start()

    slot_i = iota((n * SLOTS, n), 0)
    slot_c = iota((n * SLOTS, n), 1)
    spread = onehot(slot_c == ((slot_i >> 3) & 7) * 16 + (slot_i >> 6))
    slot_lane = slot_c == (slot_i & 7) + z * 16
    ones = jnp.ones((8, n), BF16)

    def label_forms(codes):
        every = mm(spread, codes)
        per_slot = jnp.where(slot_lane, every, 0.0)
        return every, jnp.sum(per_slot, axis=1, keepdims=True), mm_nt(ones, per_slot.astype(BF16))[0:1]

    _, col, row_own = label_forms(mz[...].reshape(n, 128))
    lab_col[...] = col
    block_i = iota((n, n), 0)
    blocks = mm(onehot(iota((n, n), 1) == (block_i & 7) * 16 + (block_i >> 3)), mz[...].reshape(n, 128))
    ecode = jnp.sum(jnp.where(iota((n, n), 1) == z * 16 + SLOTS, blocks, 0.0), axis=1, keepdims=True)
    ecode_send[...] = jnp.broadcast_to(ecode, (n, 128)).astype(BF16)
    below = (me + n - 1) % n
    edge_code_copy = remote(ecode_send, ecode_own, edge_ssem.at[5], edge_sem.at[5], below, rep)
    edge_code_copy.start()
    pair_meta.wait()
    _, _, row_sib = label_forms(mz_sib[...].reshape(n, 128))
    dens[...] = jnp.zeros((n * SLOTS, 1), F32)

    def flat(ref, begin, end):
        return ref[pl.ds(begin, end - begin)].reshape((end - begin) * SLOTS, 1024)

    def add_density(begin, end, cand, cand_labels):
        for b in range(begin, end, 32):
            e = min(b + 32, end)
            part = pl.ds(b * SLOTS, (e - b) * SLOTS)
            scores = mm_nt(flat(own, b, e), cand) * (1.0 / 1024.0)
            kept = jnp.where(lab_col[part] == cand_labels, jnp.exp(BETA * (scores - 1.0)), 0.0)
            dens[part] += jnp.sum(kept, axis=1, keepdims=True)

    def group_pair(g):
        begin, count = GROUPS[g]
        part = pl.ds(begin, count)
        return pair(own.at[part], sib.at[part], g)

    def group_edge(g):
        begin, count = GROUPS[g]
        part = pl.ds(begin, count)
        return remote(edge_send.at[part], edge_own.at[part], edge_ssem.at[g], edge_sem.at[g], below, rep)

    def arrive(g):
        begin, count = GROUPS[g]
        part = pl.ds(begin, count)
        pltpu.make_async_copy(send.at[part], own.at[part], row_sem.at[g]).wait()
        group_pair(g).start()
        first = onehot(iota((count, count * SLOTS), 1) == SLOTS * iota((count, count * SLOTS), 0))
        edge_send[part] = mm(first, flat(own, begin, begin + count)).astype(BF16)
        group_edge(g).start()

    def process(g):
        begin, count = GROUPS[g]
        end = begin + count
        new = slice(begin * SLOTS, end * SLOTS)
        seen = slice(0, end * SLOTS)
        add_density(begin, end, flat(own, 0, end), row_own[:, seen])
        if begin:
            add_density(0, begin, flat(own, begin, end), row_own[:, new])
        group_pair(g).wait()
        add_density(begin, end, flat(sib, 0, end), row_sib[:, seen])
        if begin:
            add_density(0, begin, flat(sib, begin, end), row_sib[:, new])

    for g in range(len(GROUPS)):
        arrive(g)
        if g:
            process(g - 1)
    for g in range(len(GROUPS)):
        group_edge(g).wait()
    edge_code_copy.wait()
    relay = [pair(edge_own, edge_sib, 6), pair(ecode_own, ecode_sib, 7)]
    for copy in relay:
        copy.start()
    process(len(GROUPS) - 1)
    for copy in relay:
        copy.wait()
    live = me < n - 1

    def edge_labels(ref):
        return jnp.where(live, mm_nt(onehot(iota((8, 128), 1) == 0), ref[...])[0:1], 0.0)

    add_density(0, n, edge_own[...], edge_labels(ecode_own))
    add_density(0, n, edge_sib[...], edge_labels(ecode_sib))

    weighted = (dens[...] * flat(own, 0, n).astype(F32)).astype(BF16)
    member = onehot(iota((CLUSTERS, n * SLOTS), 0) + 1 == row_own.astype(jnp.int32))
    num[...] = mm(member, weighted)
    cnt[...] = jnp.broadcast_to(jnp.sum(member.astype(F32), axis=1, keepdims=True), (CLUSTERS, 128))
    pair_num = [pair(num, num_sib, 8), pair(cnt, cnt_sib, 9)]
    for copy in pair_num:
        copy.start()
    remote(send.at[pl.ds(0, n - 1)], own.at[pl.ds(0, n - 1)], row_ssem, row_sem.at[0], me, other).wait_send()
    remote(msend.at[pl.ds(0, 15)], mplane.at[pl.ds(0, 15)], mp_ssem, mp_sem, me, other).wait_send()
    for copy in pair_num:
        copy.wait()
    ztab[0] = ((num[...] + num_sib[...]) / (cnt[:, 0:1] + cnt_sib[:, 0:1] + 1.0)).astype(BF16)

    half = pl.ds(pl.multiple_of(rep * 32, 32), 32)

    def table_copy(j):
        return remote(ztab.at[0, half], ztab.at[j, half], zt_ssem.at[j], zt_sem.at[j], chip(0, -ZO[j], 0), rep)

    def table_pair(j):
        return remote(ztab.at[j, half], ztab.at[j, half], zp_ssem.at[j], zp_sem.at[j], me, other)

    for j in range(1, 8):
        table_copy(j).start()
    cons_ref[...] = ztab[0, :, pl.ds(pl.multiple_of(rep * 512, 512), 512)]

    plane_i = iota((16 * SLOTS, 128), 0)
    plane_c = iota((16 * SLOTS, 128), 1)
    codes = mm(onehot(iota((16 * SLOTS, 16), 1) == plane_i[:, 0:16] >> 3), mz[0])

    def answer(j):
        at = ((z + ZO[j]) % 8) * 16
        labels = jnp.sum(jnp.where(plane_c == (plane_i & 7) + at, codes, 0.0), axis=1, keepdims=True)
        pick = onehot(iota((16 * SLOTS, CLUSTERS), 1) + 1 == labels.astype(jnp.int32))
        send[pl.ds(16 * j, 16)] = mm(pick, ztab[j]).reshape(16, SLOTS, 1024).astype(BF16)
        pltpu.make_async_copy(send.at[16 * j], ret.at[16 * j], ret_sem.at[j // 2]).start()

        @pl.loop(1, 16)
        def _(p):
            remote(send.at[16 * j + p], ret.at[16 * j + p], ret_ssem, ret_sem.at[j // 2],
                   chip(-(p // 4), 0, -(p % 4)), rep).start()

    for j in range(8):
        if j < 7:
            table_copy(j + 1).wait_recv()
            table_pair(j + 1).start()
        if j:
            table_pair(j).wait_recv()
        answer(j)

    for q in range(4):
        part = pl.ds(32 * q, 32)
        pltpu.make_async_copy(send.at[part], ret.at[part], ret_sem.at[q]).wait()
        pick = onehot(iota((rows, 256), 1) + 256 * q == slot_col)
        got = mm(pick, ret[part].reshape(256, 1024))
        if q == 0:
            acc[...] = got
        elif q < 3:
            acc[...] += got
        else:
            out_ref[...] = (acc[...] + got).astype(BF16)
    for j in range(1, 8):
        table_copy(j).wait_send()
        table_pair(j).wait_send()
    remote(send.at[pl.ds(0, 120)], ret.at[pl.ds(0, 120)], ret_ssem, ret_sem.at[0], me, other).wait_send()


def body(spectra, window, labels, edge_labels):
    rows, dim = spectra.shape
    n = lax.axis_size("mass")
    code = (window * 8192 + labels * 128 + edge_labels + 1).reshape(1, rows)
    vm = lambda shape, t=BF16: pltpu.VMEM(shape, t)
    block = (n, SLOTS, dim)
    dma = pltpu.SemaphoreType.DMA
    regular = pltpu.SemaphoreType.REGULAR
    return pl.pallas_call(
        kernel,
        out_shape=(
            jax.ShapeDtypeStruct((CLUSTERS, dim // 2), BF16),
            jax.ShapeDtypeStruct((rows, dim), BF16),
        ),
        in_specs=[pl.BlockSpec(memory_space=pltpu.VMEM)] * 2,
        out_specs=(pl.BlockSpec(memory_space=pltpu.VMEM), pl.BlockSpec(memory_space=pltpu.VMEM)),
        scratch_shapes=[
            vm((rows, dim)), vm(block), vm(block), vm(block), vm(block), vm((rows, dim), F32),
            vm((16, 1, 128), F32), vm((16, 1, 128), F32), vm((8, 16, 128)), vm((8, 16, 128)), vm((8, CLUSTERS, dim)),
            vm((n, dim)), vm((n, dim)), vm((n, dim)), vm((n, 128)), vm((n, 128)), vm((n, 128)),
            vm((CLUSTERS, dim), F32), vm((CLUSTERS, dim), F32), vm((CLUSTERS, 128), F32), vm((CLUSTERS, 128), F32),
            vm((n * SLOTS, 1), F32), vm((n * SLOTS, 1), F32),
            regular, regular, dma, dma((5,)), dma, dma((4,)), dma, dma, dma((8,)), dma((8,)),
            dma((10,)), dma((10,)), dma((6,)), dma((6,)), dma((8,)), dma((8,)), dma((8,)), dma((8,)),
        ],
        compiler_params=pltpu.CompilerParams(
            collective_id=0, has_side_effects=True, vmem_limit_bytes=56 * 1024 * 1024),
        cost_estimate=pl.CostEstimate(flops=8 * 10**9, bytes_accessed=4 * 10**6, transcendentals=2 * 10**6),
        name="consensus",
    )(spectra, code)


def solution(mesh):
    placed = (P(("mass", "rep"), None), P(("mass", "rep")), P(("mass", "rep")), P(("mass", "rep")))
    return jax.shard_map(
        body,
        mesh=mesh,
        in_specs=placed,
        out_specs=(P("mass", "rep"), P(("mass", "rep"), None)),
        check_vma=False,
    )
```

```python
import functools

import jax
import jax.numpy as jnp
from jax import lax
from jax.experimental import pallas as pl
from jax.experimental.pallas import tpu as pltpu
from jax.sharding import PartitionSpec as P

MESH = pl.DeviceIdType.MESH
CLUSTERS = 64
SLOTS = 8
BETA = 6.0
F32 = jnp.float32
BF16 = jnp.bfloat16
NT = (((1,), (1,)), ((), ()))


def iota(shape, dim):
    return lax.broadcasted_iota(jnp.int32, shape, dim)


def onehot(cond):
    return jnp.where(cond, 1.0, 0.0).astype(BF16)


def mm(a, b):
    return jnp.dot(a, b, preferred_element_type=F32)


def mm_nt(a, b):
    return lax.dot_general(a, b, NT, preferred_element_type=F32)


ZO = (0, 1, 7, 2, 6, 3, 5, 4)
GROUPS = ((0, 32), (32, 32), (64, 32), (96, 16), (112, 16))


def depth_of(j):
    return jnp.where(j % 2 == 1, (j + 1) // 2, (8 - j // 2) % 8)


def order_of(depth):
    return jnp.where(depth > 4, 2 * (8 - depth), jnp.maximum(2 * depth - 1, 0))


def kernel(
    x_ref, window_ref, label_ref, edge_ref, cons_ref, out_ref,
    unit, send, own, sib, ret, acc, msend, mplane, mz, mz_sib, ztab,
    edge_send, edge_in, ecode_send, ecode_in, num, num_sib, dens, lab_col, picks,
    plane_sem, row_ssem, row_sem, ret_ssem, ret_sem, mp_ssem, mp_sem, mz_ssem, mz_sem,
    pair_ssem, pair_sem, edge_ssem, edge_sem, zt_ssem, zt_sem, zp_ssem, zp_sem,
):
    me = lax.axis_index("mass")
    rep = lax.axis_index("rep")
    other = 1 - rep
    n = 128
    rows = x_ref.shape[0]
    x, z, y = me // 32, (me // 4) % 8, me % 4

    def chip(dx, dz, dy):
        return ((x + dx) % 4) * 32 + ((z + dz) % 8) * 4 + (y + dy) % 4

    def signal(sem, m, r):
        pl.semaphore_signal(sem, inc=1, device_id=(m, r), device_id_type=MESH)

    def remote(src, dst, ssem, rsem, m, r):
        return pltpu.make_async_remote_copy(
            src_ref=src, dst_ref=dst, send_sem=ssem, recv_sem=rsem, device_id=(m, r), device_id_type=MESH)

    barrier = pltpu.get_barrier_semaphore()
    for k in range(1, 8):
        signal(barrier, chip(0, k, 0), rep)
    for p in range(1, 16):
        signal(barrier, chip(p // 4, 0, p % 4), rep)
    signal(barrier, me, other)
    signal(barrier, (me + 1) % n, other)

    code_row = window_ref[...] * 8192 + label_ref[...] * 128 + edge_ref[...] + 1
    diag = iota((rows, rows), 0) == iota((rows, rows), 1)
    code_col = jnp.sum(jnp.where(diag, code_row.astype(F32), 0.0), axis=1, keepdims=True).astype(jnp.int32)

    def fields(code):
        return code >> 13, (code >> 7) & 63, code & 127

    w_row, _, e_row = fields(code_row)
    w_col, l_col, e_col = fields(code_col)
    key_row = iota((1, rows), 1) - jnp.where(e_row > 0, rows, 0)
    key_col = iota((rows, 1), 0) - jnp.where(e_col > 0, rows, 0)
    same = w_col == w_row
    rank_row = jnp.sum(jnp.where(same & (key_col < key_row), 1.0, 0.0), axis=0, keepdims=True).astype(jnp.int32)
    rank_col = jnp.sum(jnp.where(same & (key_row < key_col), 1.0, 0.0), axis=1, keepdims=True).astype(jnp.int32)

    def place(window):
        plane = (((window >> 5) - x) & 3) * 4 + ((window - y) & 3)
        return plane, order_of(((window >> 2) - z) & 7)

    plane_row, order_row = place(w_row)
    plane_col, order_col = place(w_col)
    slot_row = (plane_row * 8 + order_row) * SLOTS + rank_row
    slot_col = (order_col * 16 + plane_col) * SLOTS + rank_col

    wide = x_ref[...].astype(F32)
    unit[...] = (wide * lax.rsqrt(jnp.mean(wide * wide, axis=1, keepdims=True) + 1e-6)).astype(BF16)

    lane = iota((rows, 128), 1) - ((w_col >> 2) & 7) * 16
    code2 = jnp.where(lane == rank_col, l_col + 1, 0) + jnp.where(lane == rank_col + SLOTS, e_col, 0)
    meta = mm(onehot(iota((16, rows), 0) == plane_row), code2.astype(F32).astype(BF16))
    msend[...] = meta.reshape(16, 1, 128)

    def pack(c):
        pick = onehot(iota((256, rows), 0) + 256 * c == slot_row)
        send[pl.ds(32 * c, 32)] = mm(pick, unit[...]).reshape(32, SLOTS, 1024).astype(BF16)

    pack(0)
    pl.semaphore_wait(barrier, 24)
    for p in range(1, 16):
        signal(plane_sem, chip(p // 4, 0, p % 4), rep)

    def plane_copy(p, sign):
        return remote(msend.at[p], mplane.at[p], mp_ssem, mp_sem, chip(sign * (p // 4), 0, sign * (p % 4)), rep)

    pltpu.make_async_copy(msend.at[0], mplane.at[0], mp_sem).start()
    pltpu.make_async_copy(send.at[0], own.at[0], row_sem.at[0]).start()
    for p in range(1, 16):
        plane_copy(p, 1).start()

    def send_block(p, j, group):
        d = p * 8 + j
        remote(send.at[d], own.at[d], row_ssem, row_sem.at[group], chip(p // 4, depth_of(j), p % 4), rep).start()

    @pl.loop(1, 8)
    def _(j):
        send_block(0, j, 0)

    for c in range(1, 4):
        pack(c)
    for g, (begin, count) in enumerate(GROUPS):
        @pl.loop(max(1, begin // 8), (begin + count) // 8)
        def _(p):
            send_block(p, 0, g)

    pl.semaphore_wait(plane_sem, 15)

    def send_rows(group):
        begin, count = GROUPS[group]
        first = max(1, begin // 8)

        @pl.loop(0, 7 * ((begin + count) // 8 - first))
        def _(i):
            send_block(first + i // 7, 1 + i % 7, group)

    send_rows(0)

    pltpu.make_async_copy(msend, mplane, mp_sem).wait()
    mz[0] = mplane[...].reshape(16, 128).astype(BF16)
    for j in range(1, 8):
        remote(mz.at[0], mz.at[j], mz_ssem.at[j], mz_sem.at[j], chip(0, ZO[j], 0), rep).start()
    send_rows(1)
    send_rows(2)

    def pair(src, dst, k):
        return remote(src, dst, pair_ssem.at[k], pair_sem.at[k], me, other)

    for j in range(1, 8):
        remote(mz.at[0], mz.at[j], mz_ssem.at[j], mz_sem.at[j], chip(0, ZO[j], 0), rep).wait()
    pair_meta = pair(mz, mz_sib, 5)
    pair_meta.start()

    slot_i = iota((n * SLOTS, n), 0)
    slot_c = iota((n * SLOTS, n), 1)
    spread = onehot(slot_c == ((slot_i >> 3) & 7) * 16 + (slot_i >> 6))
    slot_lane = slot_c == (slot_i & 7) + z * 16
    ones = jnp.ones((8, n), BF16)

    def label_forms(codes):
        every = mm(spread, codes)
        per_slot = jnp.where(slot_lane, every, 0.0)
        return every, jnp.sum(per_slot, axis=1, keepdims=True), mm_nt(ones, per_slot.astype(BF16))[0:1]

    _, col, row_own = label_forms(mz[...].reshape(n, 128))
    lab_col[...] = col
    block_i = iota((n, n), 0)
    blocks = mm(onehot(iota((n, n), 1) == (block_i & 7) * 16 + (block_i >> 3)), mz[...].reshape(n, 128))
    ecode = jnp.sum(jnp.where(iota((n, n), 1) == z * 16 + SLOTS, blocks, 0.0), axis=1, keepdims=True)
    ecode_send[...] = jnp.broadcast_to(ecode, (n, 128)).astype(BF16)
    below = (me + n - 1) % n
    edge_codes = [
        remote(ecode_send, ecode_in.at[k], edge_ssem.at[k, 5], edge_sem.at[k, 5], below, r)
        for k, r in enumerate((rep, other))
    ]
    for copy in edge_codes:
        copy.start()
    pair_meta.wait()
    _, _, row_sib = label_forms(mz_sib[...].reshape(n, 128))
    dens[...] = jnp.zeros((n * SLOTS, 1), F32)
    cluster = iota((CLUSTERS, n * SLOTS), 0) + 1
    member = onehot(cluster == row_own.astype(jnp.int32))
    also = onehot(cluster == row_sib.astype(jnp.int32))
    count_all = jnp.sum(member.astype(F32) + also.astype(F32), axis=1, keepdims=True)

    plane_i = iota((16 * SLOTS, 128), 0)
    plane_c = iota((16 * SLOTS, 128), 1)
    codes = mm(onehot(iota((16 * SLOTS, 16), 1) == iota((16 * SLOTS, 16), 0) >> 3), mz[0])
    for j in range(8):
        at = ((z + ZO[j]) % 8) * 16
        labels = jnp.sum(jnp.where(plane_c == (plane_i & 7) + at, codes, 0.0), axis=1, keepdims=True)
        picks[j] = onehot(iota((16 * SLOTS, CLUSTERS), 1) + 1 == labels.astype(jnp.int32))

    def flat(ref, begin, end):
        return ref[pl.ds(begin, end - begin)].reshape((end - begin) * SLOTS, 1024)

    def add_density(begin, end, cand, cand_labels):
        for b in range(begin, end, 32):
            e = min(b + 32, end)
            part = pl.ds(b * SLOTS, (e - b) * SLOTS)
            scores = mm_nt(flat(own, b, e), cand) * (1.0 / 1024.0)
            kept = jnp.where(lab_col[part] == cand_labels, jnp.exp(BETA * (scores - 1.0)), 0.0)
            dens[part] += jnp.sum(kept, axis=1, keepdims=True)

    def group_pair(g):
        begin, count = GROUPS[g]
        part = pl.ds(begin, count)
        return pair(own.at[part], sib.at[part], g)

    def group_edge(g):
        begin, count = GROUPS[g]
        part = pl.ds(begin, count)
        return remote(edge_send.at[part], edge_in.at[0, part], edge_ssem.at[0, g], edge_sem.at[0, g], below, rep)

    def pass_edge(g):
        begin, count = GROUPS[g]
        part = pl.ds(begin, count)
        return remote(edge_in.at[0, part], edge_in.at[1, part], edge_ssem.at[1, g], edge_sem.at[1, g], me, other)

    def arrive(g):
        begin, count = GROUPS[g]
        part = pl.ds(begin, count)
        pltpu.make_async_copy(send.at[part], own.at[part], row_sem.at[g]).wait()
        group_pair(g).start()
        first = onehot(iota((count, count * SLOTS), 1) == SLOTS * iota((count, count * SLOTS), 0))
        edge_send[part] = mm(first, flat(own, begin, begin + count)).astype(BF16)
        group_edge(g).start()

    def process(g):
        begin, count = GROUPS[g]
        end = begin + count
        new = slice(begin * SLOTS, end * SLOTS)
        seen = slice(0, end * SLOTS)
        add_density(begin, end, flat(own, 0, end), row_own[:, seen])
        if begin:
            add_density(0, begin, flat(own, begin, end), row_own[:, new])
        group_edge(g).wait()
        pass_edge(g).start()
        group_pair(g).wait()
        add_density(begin, end, flat(sib, 0, end), row_sib[:, seen])
        if begin:
            add_density(0, begin, flat(sib, begin, end), row_sib[:, new])

    for g in range(len(GROUPS)):
        arrive(g)
        if g + 3 < len(GROUPS):
            send_rows(g + 3)
        if g:
            process(g - 1)
    process(len(GROUPS) - 1)
    for copy in edge_codes:
        copy.wait()
    edge_row = jnp.where(
        me < n - 1,
        mm_nt(onehot(iota((8, 128), 1) == 0), ecode_in[...].reshape(2 * n, 128))[0:1], 0.0)
    for g in range(len(GROUPS)):
        pass_edge(g).wait()
    add_density(0, n, edge_in[...].reshape(2 * n, 1024), edge_row)

    weighted = (dens[...] * flat(own, 0, n).astype(F32)).astype(BF16)
    num[...] = mm(member, weighted)
    pair_num = pair(num, num_sib, 6)
    pair_num.start()
    remote(send.at[pl.ds(0, n - 1)], own.at[pl.ds(0, n - 1)], row_ssem, row_sem.at[0], me, other).wait_send()
    remote(msend.at[pl.ds(0, 15)], mplane.at[pl.ds(0, 15)], mp_ssem, mp_sem, me, other).wait_send()
    pair_num.wait()
    ztab[0] = ((num[...] + num_sib[...]) / (count_all + 1.0)).astype(BF16)

    half = pl.ds(pl.multiple_of(rep * 32, 32), 32)

    def table_copy(j):
        src, dst = (ztab.at[0], ztab.at[j]) if j < 3 else (ztab.at[0, half], ztab.at[j, half])
        return remote(src, dst, zt_ssem.at[j], zt_sem.at[j], chip(0, -ZO[j], 0), rep)

    def table_pair(j):
        return remote(ztab.at[j, half], ztab.at[j, half], zp_ssem.at[j], zp_sem.at[j], me, other)

    for j in range(1, 8):
        table_copy(j).start()
    cons_ref[...] = ztab[0, :, pl.ds(pl.multiple_of(rep * 512, 512), 512)]

    def answer(j):
        send[pl.ds(16 * j, 16)] = mm(picks[j], ztab[j]).reshape(16, SLOTS, 1024).astype(BF16)
        pltpu.make_async_copy(send.at[16 * j], ret.at[16 * j], ret_sem.at[j // 2]).start()

        @pl.loop(1, 16)
        def _(p):
            remote(send.at[16 * j + p], ret.at[16 * j + p], ret_ssem, ret_sem.at[j // 2],
                   chip(-(p // 4), 0, -(p % 4)), rep).start()

    for j in range(8):
        if j in (1, 2):
            table_copy(j).wait_recv()
        elif j:
            table_pair(j).wait_recv()
        answer(j)
        k = j + 2
        if 3 <= k < 8:
            table_copy(k).wait_recv()
            table_pair(k).start()

    for q in range(4):
        part = pl.ds(32 * q, 32)
        pick = onehot(iota((rows, 256), 1) + 256 * q == slot_col)
        pltpu.make_async_copy(send.at[part], ret.at[part], ret_sem.at[q]).wait()
        got = mm(pick, ret[part].reshape(256, 1024))
        if q == 0:
            acc[...] = got
        elif q < 3:
            acc[...] += got
        else:
            out_ref[...] = (acc[...] + got).astype(BF16)
    for j in range(1, 8):
        table_copy(j).wait_send()
        if j >= 3:
            table_pair(j).wait_send()
    remote(send.at[pl.ds(0, 120)], ret.at[pl.ds(0, 120)], ret_ssem, ret_sem.at[0], me, other).wait_send()


def body(spectra, window, labels, edge_labels):
    rows, dim = spectra.shape
    n = lax.axis_size("mass")
    vm = lambda shape, t=BF16: pltpu.VMEM(shape, t)
    block = (n, SLOTS, dim)
    dma = pltpu.SemaphoreType.DMA
    regular = pltpu.SemaphoreType.REGULAR
    cons, assigned = pl.pallas_call(
        kernel,
        out_shape=(
            jax.ShapeDtypeStruct((CLUSTERS, dim // 2), BF16),
            jax.ShapeDtypeStruct((rows, dim), BF16),
        ),
        in_specs=[pl.BlockSpec(memory_space=pltpu.VMEM)] * 4,
        out_specs=(pl.BlockSpec(memory_space=pltpu.VMEM), pl.BlockSpec(memory_space=pltpu.VMEM)),
        scratch_shapes=[
            vm((rows, dim)), vm(block), vm(block), vm(block), vm(block), vm((rows, dim), F32),
            vm((16, 1, 128), F32), vm((16, 1, 128), F32), vm((8, 16, 128)), vm((8, 16, 128)), vm((8, CLUSTERS, dim)),
            vm((n, dim)), vm((2, n, dim)), vm((n, 128)), vm((2, n, 128)),
            vm((CLUSTERS, dim), F32), vm((CLUSTERS, dim), F32), vm((n * SLOTS, 1), F32), vm((n * SLOTS, 1), F32),
            vm((8, 16 * SLOTS, CLUSTERS)),
            regular, dma, dma((5,)), dma, dma((4,)), dma, dma, dma((8,)), dma((8,)),
            dma((7,)), dma((7,)), dma((2, 6)), dma((2, 6)), dma((8,)), dma((8,)), dma((8,)), dma((8,)),
        ],
        compiler_params=pltpu.CompilerParams(
            collective_id=0, has_side_effects=True, vmem_limit_bytes=56 * 1024 * 1024),
        cost_estimate=pl.CostEstimate(flops=8 * 10**9, bytes_accessed=4 * 10**6, transcendentals=2 * 10**6),
        name="consensus",
    )(spectra, window.reshape(1, rows), labels.reshape(1, rows), edge_labels.reshape(1, rows))
    return pl.pallas_call(
        place,
        out_shape=(jax.ShapeDtypeStruct(cons.shape, BF16), jax.ShapeDtypeStruct(assigned.shape, BF16)),
        in_specs=[pl.BlockSpec(memory_space=pltpu.VMEM)] * 2,
        out_specs=(pl.BlockSpec(memory_space=pltpu.VMEM), pl.BlockSpec(memory_space=pltpu.VMEM)),
        name="place",
    )(cons, assigned)


def place(a_ref, b_ref, c_ref, d_ref):
    c_ref[...] = a_ref[...]
    d_ref[...] = b_ref[...]


def solution(mesh):
    placed = (P(("mass", "rep"), None), P(("mass", "rep")), P(("mass", "rep")), P(("mass", "rep")))
    return jax.shard_map(
        body,
        mesh=mesh,
        in_specs=placed,
        out_specs=(P("mass", "rep"), P(("mass", "rep"), None)),
        check_vma=False,
    )
```

```python
import functools

import jax
import jax.numpy as jnp
from jax import lax
from jax.experimental import pallas as pl
from jax.experimental.pallas import tpu as pltpu
from jax.sharding import PartitionSpec as P

MESH = pl.DeviceIdType.MESH
CLUSTERS = 64
SLOTS = 8
BETA = 6.0
F32 = jnp.float32
BF16 = jnp.bfloat16
NT = (((1,), (1,)), ((), ()))


def iota(shape, dim):
    return lax.broadcasted_iota(jnp.int32, shape, dim)


def onehot(cond):
    return jnp.where(cond, 1.0, 0.0).astype(BF16)


def mm(a, b):
    return jnp.dot(a, b, preferred_element_type=F32)


def mm_nt(a, b):
    return lax.dot_general(a, b, NT, preferred_element_type=F32)


ZO = (0, 1, 7, 2, 6, 3, 5, 4)
GROUPS = ((0, 32), (32, 32), (64, 32), (96, 16), (112, 16))


def depth_of(j):
    return jnp.where(j % 2 == 1, (j + 1) // 2, (8 - j // 2) % 8)


def order_of(depth):
    return jnp.where(depth > 4, 2 * (8 - depth), jnp.maximum(2 * depth - 1, 0))


def kernel(
    x_ref, window_ref, label_ref, edge_ref, cons_ref, out_ref,
    unit, send, own, sib, ret, acc, msend, mplane, mz, mz_sib, ztab,
    edge_send, edge_in, ecode_send, ecode_in, num, num_sib, dens, lab_col, picks,
    plane_sem, row_ssem, row_sem, ret_ssem, ret_sem, mp_ssem, mp_sem, mz_ssem, mz_sem,
    pair_ssem, pair_sem, edge_ssem, edge_sem, zt_ssem, zt_sem, zp_ssem, zp_sem,
):
    me = lax.axis_index("mass")
    rep = lax.axis_index("rep")
    other = 1 - rep
    n = 128
    rows = x_ref.shape[0]
    x, z, y = me // 32, (me // 4) % 8, me % 4

    def chip(dx, dz, dy):
        return ((x + dx) % 4) * 32 + ((z + dz) % 8) * 4 + (y + dy) % 4

    def signal(sem, m, r):
        pl.semaphore_signal(sem, inc=1, device_id=(m, r), device_id_type=MESH)

    def remote(src, dst, ssem, rsem, m, r):
        return pltpu.make_async_remote_copy(
            src_ref=src, dst_ref=dst, send_sem=ssem, recv_sem=rsem, device_id=(m, r), device_id_type=MESH)

    barrier = pltpu.get_barrier_semaphore()
    for k in range(1, 8):
        signal(barrier, chip(0, k, 0), rep)
    for p in range(1, 16):
        signal(barrier, chip(p // 4, 0, p % 4), rep)
    signal(barrier, me, other)
    signal(barrier, (me + 1) % n, other)

    code_row = window_ref[...] * 8192 + label_ref[...] * 128 + edge_ref[...] + 1
    diag = iota((rows, rows), 0) == iota((rows, rows), 1)
    code_col = jnp.sum(jnp.where(diag, code_row.astype(F32), 0.0), axis=1, keepdims=True).astype(jnp.int32)

    def fields(code):
        return code >> 13, (code >> 7) & 63, code & 127

    w_row, _, e_row = fields(code_row)
    w_col, l_col, e_col = fields(code_col)
    key_row = iota((1, rows), 1) - jnp.where(e_row > 0, rows, 0)
    key_col = iota((rows, 1), 0) - jnp.where(e_col > 0, rows, 0)
    same = w_col == w_row
    rank_row = jnp.sum(jnp.where(same & (key_col < key_row), 1.0, 0.0), axis=0, keepdims=True).astype(jnp.int32)
    rank_col = jnp.sum(jnp.where(same & (key_row < key_col), 1.0, 0.0), axis=1, keepdims=True).astype(jnp.int32)

    def place(window):
        plane = (((window >> 5) - x) & 3) * 4 + ((window - y) & 3)
        return plane, order_of(((window >> 2) - z) & 7)

    plane_row, order_row = place(w_row)
    plane_col, order_col = place(w_col)
    slot_row = (plane_row * 8 + order_row) * SLOTS + rank_row
    slot_col = (order_col * 16 + plane_col) * SLOTS + rank_col

    wide = x_ref[...].astype(F32)
    unit[...] = (wide * lax.rsqrt(jnp.mean(wide * wide, axis=1, keepdims=True) + 1e-6)).astype(BF16)

    lane = iota((rows, 128), 1) - ((w_col >> 2) & 7) * 16
    code2 = jnp.where(lane == rank_col, l_col + 1, 0) + jnp.where(lane == rank_col + SLOTS, e_col, 0)
    meta = mm(onehot(iota((16, rows), 0) == plane_row), code2.astype(F32).astype(BF16))
    msend[...] = meta.reshape(16, 1, 128)

    def pack(c):
        pick = onehot(iota((256, rows), 0) + 256 * c == slot_row)
        send[pl.ds(32 * c, 32)] = mm(pick, unit[...]).reshape(32, SLOTS, 1024).astype(BF16)

    pack(0)
    pl.semaphore_wait(barrier, 24)
    for p in range(1, 16):
        signal(plane_sem, chip(p // 4, 0, p % 4), rep)

    def plane_copy(p, sign):
        return remote(msend.at[p], mplane.at[p], mp_ssem, mp_sem, chip(sign * (p // 4), 0, sign * (p % 4)), rep)

    pltpu.make_async_copy(msend.at[0], mplane.at[0], mp_sem).start()
    pltpu.make_async_copy(send.at[0], own.at[0], row_sem.at[0]).start()
    for p in range(1, 16):
        plane_copy(p, 1).start()

    def send_block(p, j, group):
        d = p * 8 + j
        remote(send.at[d], own.at[d], row_ssem, row_sem.at[group], chip(p // 4, depth_of(j), p % 4), rep).start()

    @pl.loop(1, 8)
    def _(j):
        send_block(0, j, 0)

    for c in range(1, 4):
        pack(c)
    for g, (begin, count) in enumerate(GROUPS):
        @pl.loop(max(1, begin // 8), (begin + count) // 8)
        def _(p):
            send_block(p, 0, g)

    pl.semaphore_wait(plane_sem, 15)

    def send_rows(group):
        begin, count = GROUPS[group]
        first = max(1, begin // 8)

        @pl.loop(0, 7 * ((begin + count) // 8 - first))
        def _(i):
            send_block(first + i // 7, 1 + i % 7, group)

    send_rows(0)

    pltpu.make_async_copy(msend, mplane, mp_sem).wait()
    mz[0] = mplane[...].reshape(16, 128).astype(BF16)
    for j in range(1, 8):
        remote(mz.at[0], mz.at[j], mz_ssem.at[j], mz_sem.at[j], chip(0, ZO[j], 0), rep).start()
    send_rows(1)
    send_rows(2)

    def pair(src, dst, k):
        return remote(src, dst, pair_ssem.at[k], pair_sem.at[k], me, other)

    for j in range(1, 8):
        remote(mz.at[0], mz.at[j], mz_ssem.at[j], mz_sem.at[j], chip(0, ZO[j], 0), rep).wait()
    pair_meta = pair(mz, mz_sib, 5)
    pair_meta.start()

    slot_i = iota((n * SLOTS, n), 0)
    slot_c = iota((n * SLOTS, n), 1)
    spread = onehot(slot_c == ((slot_i >> 3) & 7) * 16 + (slot_i >> 6))
    slot_lane = slot_c == (slot_i & 7) + z * 16
    ones = jnp.ones((8, n), BF16)

    def label_forms(codes):
        every = mm(spread, codes)
        per_slot = jnp.where(slot_lane, every, 0.0)
        return every, jnp.sum(per_slot, axis=1, keepdims=True), mm_nt(ones, per_slot.astype(BF16))[0:1]

    _, col, row_own = label_forms(mz[...].reshape(n, 128))
    lab_col[...] = col
    block_i = iota((n, n), 0)
    blocks = mm(onehot(iota((n, n), 1) == (block_i & 7) * 16 + (block_i >> 3)), mz[...].reshape(n, 128))
    ecode = jnp.sum(jnp.where(iota((n, n), 1) == z * 16 + SLOTS, blocks, 0.0), axis=1, keepdims=True)
    ecode_send[...] = jnp.broadcast_to(ecode, (n, 128)).astype(BF16)
    below = (me + n - 1) % n
    edge_codes = [
        remote(ecode_send, ecode_in.at[k], edge_ssem.at[k, 5], edge_sem.at[k, 5], below, r)
        for k, r in enumerate((rep, other))
    ]
    for copy in edge_codes:
        copy.start()
    pair_meta.wait()
    _, _, row_sib = label_forms(mz_sib[...].reshape(n, 128))
    dens[...] = jnp.zeros((n * SLOTS, 1), F32)
    cluster = iota((CLUSTERS, n * SLOTS), 0) + 1
    member = onehot(cluster == row_own.astype(jnp.int32))
    also = onehot(cluster == row_sib.astype(jnp.int32))
    count_all = jnp.sum(member.astype(F32) + also.astype(F32), axis=1, keepdims=True)

    plane_i = iota((16 * SLOTS, 128), 0)
    plane_c = iota((16 * SLOTS, 128), 1)
    codes = mm(onehot(iota((16 * SLOTS, 16), 1) == iota((16 * SLOTS, 16), 0) >> 3), mz[0])
    for j in range(8):
        at = ((z + ZO[j]) % 8) * 16
        labels = jnp.sum(jnp.where(plane_c == (plane_i & 7) + at, codes, 0.0), axis=1, keepdims=True)
        picks[j] = onehot(iota((16 * SLOTS, CLUSTERS), 1) + 1 == labels.astype(jnp.int32))

    def flat(ref, begin, end):
        return ref[pl.ds(begin, end - begin)].reshape((end - begin) * SLOTS, 1024)

    def add_density(begin, end, cand, cand_labels):
        for b in range(begin, end, 32):
            e = min(b + 32, end)
            part = pl.ds(b * SLOTS, (e - b) * SLOTS)
            scores = mm_nt(flat(own, b, e), cand) * (1.0 / 1024.0)
            kept = jnp.where(lab_col[part] == cand_labels, jnp.exp(BETA * (scores - 1.0)), 0.0)
            dens[part] += jnp.sum(kept, axis=1, keepdims=True)

    def group_pair(g):
        begin, count = GROUPS[g]
        part = pl.ds(begin, count)
        return pair(own.at[part], sib.at[part], g)

    def group_edge(g):
        begin, count = GROUPS[g]
        part = pl.ds(begin, count)
        return remote(edge_send.at[part], edge_in.at[0, part], edge_ssem.at[0, g], edge_sem.at[0, g], below, rep)

    def pass_edge(g):
        begin, count = GROUPS[g]
        part = pl.ds(begin, count)
        return remote(edge_in.at[0, part], edge_in.at[1, part], edge_ssem.at[1, g], edge_sem.at[1, g], me, other)

    def arrive(g):
        begin, count = GROUPS[g]
        part = pl.ds(begin, count)
        pltpu.make_async_copy(send.at[part], own.at[part], row_sem.at[g]).wait()
        group_pair(g).start()
        first = onehot(iota((count, count * SLOTS), 1) == SLOTS * iota((count, count * SLOTS), 0))
        edge_send[part] = mm(first, flat(own, begin, begin + count)).astype(BF16)
        group_edge(g).start()

    def process(g):
        begin, count = GROUPS[g]
        end = begin + count
        new = slice(begin * SLOTS, end * SLOTS)
        seen = slice(0, end * SLOTS)
        add_density(begin, end, flat(own, 0, end), row_own[:, seen])
        if begin:
            add_density(0, begin, flat(own, begin, end), row_own[:, new])
        group_edge(g).wait()
        pass_edge(g).start()
        group_pair(g).wait()
        add_density(begin, end, flat(sib, 0, end), row_sib[:, seen])
        if begin:
            add_density(0, begin, flat(sib, begin, end), row_sib[:, new])

    for g in range(len(GROUPS)):
        arrive(g)
        if g + 3 < len(GROUPS):
            send_rows(g + 3)
        if g:
            process(g - 1)
    process(len(GROUPS) - 1)
    for copy in edge_codes:
        copy.wait()
    edge_row = jnp.where(
        me < n - 1,
        mm_nt(onehot(iota((8, 128), 1) == 0), ecode_in[...].reshape(2 * n, 128))[0:1], 0.0)
    for g in range(len(GROUPS)):
        pass_edge(g).wait()
    add_density(0, n, edge_in[...].reshape(2 * n, 1024), edge_row)

    sums = []
    for h in range(2):
        lanes = pl.ds(512 * h, 512)
        weighted = (dens[...] * own[:, :, lanes].reshape(n * SLOTS, 512).astype(F32)).astype(BF16)
        num[:, lanes] = mm(member, weighted)
        copy = pair(num.at[:, lanes], num_sib.at[:, lanes], 6 + h)
        copy.start()
        sums.append(copy)
    remote(send.at[pl.ds(0, n - 1)], own.at[pl.ds(0, n - 1)], row_ssem, row_sem.at[0], me, other).wait_send()
    remote(msend.at[pl.ds(0, 15)], mplane.at[pl.ds(0, 15)], mp_ssem, mp_sem, me, other).wait_send()
    for h, copy in enumerate(sums):
        lanes = pl.ds(512 * h, 512)
        copy.wait()
        ztab[0, :, lanes] = ((num[:, lanes] + num_sib[:, lanes]) / (count_all + 1.0)).astype(BF16)

    half = pl.ds(pl.multiple_of(rep * 32, 32), 32)

    def table_copy(j):
        src, dst = (ztab.at[0], ztab.at[j]) if j < 3 else (ztab.at[0, half], ztab.at[j, half])
        return remote(src, dst, zt_ssem.at[j], zt_sem.at[j], chip(0, -ZO[j], 0), rep)

    def table_pair(j):
        return remote(ztab.at[j, half], ztab.at[j, half], zp_ssem.at[j], zp_sem.at[j], me, other)

    for j in range(1, 8):
        table_copy(j).start()
    cons_ref[...] = ztab[0, :, pl.ds(pl.multiple_of(rep * 512, 512), 512)]

    def answer(j):
        send[pl.ds(16 * j, 16)] = mm(picks[j], ztab[j]).reshape(16, SLOTS, 1024).astype(BF16)
        pltpu.make_async_copy(send.at[16 * j], ret.at[16 * j], ret_sem.at[j // 2]).start()

        @pl.loop(1, 16)
        def _(p):
            remote(send.at[16 * j + p], ret.at[16 * j + p], ret_ssem, ret_sem.at[j // 2],
                   chip(-(p // 4), 0, -(p % 4)), rep).start()

    for j in range(8):
        if j in (1, 2):
            table_copy(j).wait_recv()
        elif j:
            table_pair(j).wait_recv()
        answer(j)
        k = j + 2
        if 3 <= k < 8:
            table_copy(k).wait_recv()
            table_pair(k).start()

    for q in range(4):
        part = pl.ds(32 * q, 32)
        pick = onehot(iota((rows, 256), 1) + 256 * q == slot_col)
        pltpu.make_async_copy(send.at[part], ret.at[part], ret_sem.at[q]).wait()
        got = mm(pick, ret[part].reshape(256, 1024))
        if q == 0:
            acc[...] = got
        elif q < 3:
            acc[...] += got
        else:
            out_ref[...] = (acc[...] + got).astype(BF16)
    for j in range(1, 8):
        table_copy(j).wait_send()
        if j >= 3:
            table_pair(j).wait_send()
    remote(send.at[pl.ds(0, 120)], ret.at[pl.ds(0, 120)], ret_ssem, ret_sem.at[0], me, other).wait_send()


def body(spectra, window, labels, edge_labels):
    rows, dim = spectra.shape
    n = lax.axis_size("mass")
    vm = lambda shape, t=BF16: pltpu.VMEM(shape, t)
    block = (n, SLOTS, dim)
    dma = pltpu.SemaphoreType.DMA
    regular = pltpu.SemaphoreType.REGULAR
    cons, assigned = pl.pallas_call(
        kernel,
        out_shape=(
            jax.ShapeDtypeStruct((CLUSTERS, dim // 2), BF16),
            jax.ShapeDtypeStruct((rows, dim), BF16),
        ),
        in_specs=[pl.BlockSpec(memory_space=pltpu.VMEM)] * 4,
        out_specs=(pl.BlockSpec(memory_space=pltpu.VMEM), pl.BlockSpec(memory_space=pltpu.VMEM)),
        scratch_shapes=[
            vm((rows, dim)), vm(block), vm(block), vm(block), vm(block), vm((rows, dim), F32),
            vm((16, 1, 128), F32), vm((16, 1, 128), F32), vm((8, 16, 128)), vm((8, 16, 128)), vm((8, CLUSTERS, dim)),
            vm((n, dim)), vm((2, n, dim)), vm((n, 128)), vm((2, n, 128)),
            vm((CLUSTERS, dim), F32), vm((CLUSTERS, dim), F32), vm((n * SLOTS, 1), F32), vm((n * SLOTS, 1), F32),
            vm((8, 16 * SLOTS, CLUSTERS)),
            regular, dma, dma((5,)), dma, dma((4,)), dma, dma, dma((8,)), dma((8,)),
            dma((8,)), dma((8,)), dma((2, 6)), dma((2, 6)), dma((8,)), dma((8,)), dma((8,)), dma((8,)),
        ],
        compiler_params=pltpu.CompilerParams(
            collective_id=0, has_side_effects=True, vmem_limit_bytes=56 * 1024 * 1024),
        cost_estimate=pl.CostEstimate(flops=8 * 10**9, bytes_accessed=4 * 10**6, transcendentals=2 * 10**6),
        name="consensus",
    )(spectra, window.reshape(1, rows), labels.reshape(1, rows), edge_labels.reshape(1, rows))
    return pl.pallas_call(
        place,
        out_shape=(jax.ShapeDtypeStruct(cons.shape, BF16), jax.ShapeDtypeStruct(assigned.shape, BF16)),
        in_specs=[pl.BlockSpec(memory_space=pltpu.VMEM)] * 2,
        out_specs=(pl.BlockSpec(memory_space=pltpu.VMEM), pl.BlockSpec(memory_space=pltpu.VMEM)),
        name="place",
    )(cons, assigned)


def place(a_ref, b_ref, c_ref, d_ref):
    c_ref[...] = a_ref[...]
    d_ref[...] = b_ref[...]


def solution(mesh):
    placed = (P(("mass", "rep"), None), P(("mass", "rep")), P(("mass", "rep")), P(("mass", "rep")))
    return jax.shard_map(
        body,
        mesh=mesh,
        in_specs=placed,
        out_specs=(P("mass", "rep"), P(("mass", "rep"), None)),
        check_vma=False,
    )
```
